256 devices in a mesh: batch: 4 (over x), pool: 32 (over z, y), tensor: 2 (over core).
Axes of the slice: x: 4, y: 4, z: 8, core: 2. Of those that a mesh axis runs over, the one named last changes fastest.
Arguments:
- hidden: bfloat16 [8192, 8192], P(('batch', 'pool'), 'tensor'), may hold values from -6 to 6
- query_base: bfloat16 [8192, 8192], P(('batch', 'pool'), 'tensor'), may hold values from -6 to 6
- new_kv: bfloat16 [8192, 2, 1024], P(('batch', 'pool'), None, 'tensor'), may hold values from -6 to 6
- cache_keys: bfloat16 [8192, 8, 64, 128], P(('batch', 'pool'), 'tensor'), may hold values from -100 to 100
- cache_values: bfloat16 [8192, 8, 64, 128], P(('batch', 'pool'), 'tensor'), may hold values from -6 to 6
- lengths: int32 [8192], P(('batch', 'pool')), may hold values from 1 to 64
- adapter_ids: int32 [2048, 1], P(('batch', 'pool')), may hold values from 0 to 31; in each aligned block of 16 rows (0 to 15, 16 to 31, ...) no two rows name the same one
- adapter_down: bfloat16 [32, 8192, 64], P('pool', 'tensor'), may hold values from -0.0625 to 0.0625
- adapter_up: bfloat16 [32, 64, 8192], P('pool', None, 'tensor'), may hold values from -0.75 to 0.75
Outputs:
- attention: bfloat16 [8192, 8192], P(('batch', 'pool'), 'tensor')
The draws below stay inside these ranges and needn't reach their ends.
Inputs may be any that keep to these rules, and one draw needn't show every extreme that they name: `adapter_ids`: within the 16 blocks of one device no adapter is named by more than 1 block.
All inputs are finite; a program needn't handle non-finite values.
Results may differ from the reference program's by a relative error of at most 0.011.
Values may be sent and summed in bfloat16 or wider, within the bound.
A program may use at most 128 MiB of HBM per device.

```python
import math
import jax
import jax.numpy as jnp
import numpy as np
from jax import lax

MODEL_WIDTH = 8192
HEADS = 64
KEY_VALUE_HEADS = 8
HEAD_SIZE = 128
RANK = 64
BLOCK = 4
BLK_DEV = 16
CACHE = 64
MOST = 1
REQUEST_TOTAL = 8192
BLOCKS = 2048
ADAPTERS = 32


def draw_cache_keys(key, part):
    key = jax.random.fold_in(key, 11)
    base_key = jax.random.fold_in(key, 0)
    shape = (REQUEST_TOTAL, KEY_VALUE_HEADS, CACHE, HEAD_SIZE)
    drawn = jax.random.normal(base_key, shape, jnp.float32)
    return jnp.clip(drawn, -6.0, 6.0).astype(jnp.bfloat16)


def draw_lengths(key, part):
    key = jax.random.fold_in(key, 23)
    drawn = jax.random.randint(key, (REQUEST_TOTAL,), 1, CACHE + 1)
    return drawn.at[0].set(CACHE).astype(jnp.int32)


def steps_of(rng, dims, pieces, low, largest):
    def one(axis_at, parts):
        heights = jax.random.uniform(jax.random.fold_in(jax.random.fold_in(rng, 6), axis_at), (parts,), jnp.float32, low / len(pieces), largest / len(pieces))
        return jnp.repeat(jnp.exp(heights), dims[axis_at] // parts).reshape((-1,) + (1,) * (len(dims) - axis_at - 1))

    level = one(*pieces[0])
    for cut in pieces[1:]:
        level = level * one(*cut)
    return level


def deal_out(rng, own, number, rows, amount, top, reach, skew):
    ranking = jax.random.permutation(rng, amount)
    heavy_load, common = load_shares(amount, rows * top, reach, skew, True), load_shares(amount, rows * top, reach, skew, False)
    places = jnp.arange(amount)

    def named(tallies, rotation):
        used = int((tallies > 0).sum())
        fixed = max(1, used // 4)
        shifted = fixed + (places - fixed + rotation * (used - fixed)) % max(1, amount - fixed)
        return jnp.zeros((amount,), jnp.int32).at[ranking[jnp.where(places < fixed, places, shifted)]].set(jnp.asarray(tallies, jnp.int32))

    tallies = jnp.where(number % 4 == 0, named(heavy_load, number // 4), named(common, number - number // 4 - 1))
    mixed = jax.random.permutation(jax.random.fold_in(own, 3), amount)
    giver, sink = mixed[0:amount // 2 * 2:2], mixed[1:amount // 2 * 2:2]
    margin = jnp.minimum(tallies[giver] - 1, reach - tallies[sink]) // 2
    margin = jnp.where((giver == ranking[0]) | (sink == ranking[0]) | (tallies[sink] == 0), 0, jnp.maximum(margin, 0))
    shifted = jax.random.randint(jax.random.fold_in(own, 4), (amount // 2,), 0, 1 << 20) % (margin + 1)
    tallies = tallies.at[giver].add(-shifted).at[sink].add(shifted)
    members = jnp.searchsorted(jnp.cumsum(tallies), jnp.arange(rows * top), side="right").astype(jnp.int32)
    listing = members.reshape(top, rows).T
    listing = listing[jax.random.permutation(jax.random.fold_in(own, 1), rows)]
    rotation = jax.random.randint(jax.random.fold_in(own, 2), (rows, 1), 0, top)
    return jnp.take_along_axis(listing, (jnp.arange(top)[None, :] + rotation) % top, axis=1)


def load_shares(number_of, total, reach, lean, full):
    loads = [(1 << 20) // math.isqrt(standing ** lean) + 1 for standing in range(1, number_of + 1)]
    largest = reach if full else min(reach, max(-(-total // number_of), total * loads[0] // sum(loads)))
    least = 1 if total - largest >= number_of - 1 else 0
    given, rest = [largest] + [least] * (number_of - 1), total - largest - least * (number_of - 1)
    while rest > 0:
        candidates = [i for i in range(1, number_of) if given[i] < largest] or [i for i in range(1, number_of) if given[i] < reach]
        pool, left = sum([loads[i] for i in candidates]), rest
        for i in candidates:
            addition = min(reach - given[i], max(1, left * loads[i] // pool), rest)
            given[i] = given[i] + addition
            rest = rest - addition
    return np.array(given)


def scatter_about(stream_key, extent, width, limit, pieces=(), dtype=jnp.bfloat16):
    level = steps_of(stream_key, extent, pieces, -0.22, 0.18) if pieces else 1.0
    values = jax.random.normal(stream_key, extent, jnp.float32) * width * level
    return jnp.minimum(jnp.maximum(values, -limit), limit).astype(dtype)


def setup_inputs(seed: int = 0) -> dict:
    keys = jax.random.split(jax.random.key(seed), 10)
    hidden = scatter_about(keys[0], (REQUEST_TOTAL, MODEL_WIDTH), 1.0, 6.0, ((0, 128), (1, 2)))
    query_base = scatter_about(keys[1], (REQUEST_TOTAL, MODEL_WIDTH), 1.0, 6.0, ((0, 128), (1, 2)))
    new_kv = scatter_about(keys[2], (REQUEST_TOTAL, 2, KEY_VALUE_HEADS * HEAD_SIZE), 1.0, 6.0, ((0, 128), (2, 2)))
    cache_keys = draw_cache_keys(jax.random.fold_in(keys[9], 71), 0)
    cache_values = scatter_about(keys[4], (REQUEST_TOTAL, KEY_VALUE_HEADS, CACHE, HEAD_SIZE), 1.0, 6.0, ((0, 128), (1, 2)))
    lengths = draw_lengths(jax.random.fold_in(keys[9], 71), 0)
    adapter_ids_keys = jax.random.split(jax.random.fold_in(keys[6], 1), BLOCKS // BLK_DEV)
    adapter_ids_turns = jax.random.permutation(jax.random.fold_in(keys[6], 3), BLOCKS // BLK_DEV)
    adapter_ids = jax.vmap(lambda own, number: deal_out(jax.random.fold_in(keys[6], 2), own, number, BLK_DEV, ADAPTERS, 1, MOST, 2))(adapter_ids_keys, adapter_ids_turns).reshape((BLOCKS, 1))
    adapter_down = scatter_about(keys[7], (ADAPTERS, MODEL_WIDTH, RANK), MODEL_WIDTH ** -0.5, 0.0625, ((0, 32), (1, 2)))
    adapter_up = scatter_about(keys[8], (ADAPTERS, RANK, MODEL_WIDTH), RANK ** -0.5, 0.75, ((0, 32), (2, 2)))
    return dict(hidden=hidden, query_base=query_base, new_kv=new_kv, cache_keys=cache_keys, cache_values=cache_values, lengths=lengths, adapter_ids=adapter_ids, adapter_down=adapter_down, adapter_up=adapter_up)


def attend_one(inputs):
    base_row, delta_row, fresh_row, key_rows, value_rows, length_row = inputs
    score_scale = 1.0 / math.sqrt(HEAD_SIZE)
    keys_wide = key_rows.astype(jnp.float32)
    values_wide = value_rows.astype(jnp.float32)
    base_wide = base_row.astype(jnp.float32)
    delta_wide = delta_row.astype(jnp.float32)
    fresh_keys = fresh_row[0].reshape(KEY_VALUE_HEADS, HEAD_SIZE).astype(jnp.float32)
    fresh_values = fresh_row[1].reshape(KEY_VALUE_HEADS, HEAD_SIZE).astype(jnp.float32)
    cached = (jnp.einsum('hgd,hld->hgl', base_wide, keys_wide) + jnp.einsum('hgd,hld->hgl', delta_wide, keys_wide)) * score_scale
    fresh = (jnp.einsum('hgd,hd->hg', base_wide, fresh_keys) + jnp.einsum('hgd,hd->hg', delta_wide, fresh_keys)) * score_scale
    valid_mask = (jnp.arange(CACHE) < length_row)[None, None, :]
    masked_scores = jnp.where(valid_mask, cached, -1e+30)
    row_max = jnp.maximum(lax.optimization_barrier(jnp.max(masked_scores, axis=2)), fresh)
    cached_exp = jnp.where(valid_mask, jnp.exp(masked_scores - row_max[:, :, None]), 0.0)
    fresh_exp = jnp.exp(fresh - row_max)
    row_total = lax.optimization_barrier(jnp.sum(cached_exp, axis=2)) + fresh_exp
    cached_weights = (cached_exp / row_total[:, :, None]).astype(jnp.bfloat16).astype(jnp.float32)
    fresh_weights = (fresh_exp / row_total).astype(jnp.bfloat16).astype(jnp.float32)
    mixed = jnp.einsum('hgl,hld->hgd', cached_weights, values_wide)
    mixed = mixed + fresh_weights[:, :, None] * fresh_values[:, None, :]
    return mixed.astype(jnp.bfloat16)

def reference(hidden, query_base, new_kv, cache_keys, cache_values, lengths, adapter_ids, adapter_down, adapter_up):
    group_width = HEADS // KEY_VALUE_HEADS
    row_index_list = jnp.broadcast_to(adapter_ids[:, 0][:, None], (BLOCKS, BLOCK)).reshape(REQUEST_TOTAL)
    lowrank = jnp.zeros((REQUEST_TOTAL, RANK), jnp.float32)
    for adapter_choice in range(ADAPTERS):
        dot_product = jnp.dot(hidden, adapter_down[adapter_choice], preferred_element_type=jnp.float32)
        lowrank = jnp.where((row_index_list == adapter_choice)[:, None], dot_product, lowrank)
    lowrank = lowrank.astype(jnp.bfloat16)
    adapter_change = jnp.zeros((REQUEST_TOTAL, MODEL_WIDTH), jnp.float32)
    for adapter_choice in range(ADAPTERS):
        dot_product = jnp.dot(lowrank, adapter_up[adapter_choice], preferred_element_type=jnp.float32)
        adapter_change = jnp.where((row_index_list == adapter_choice)[:, None], dot_product, adapter_change)
    adapter_change = adapter_change.astype(jnp.bfloat16)
    base_query = query_base.reshape(REQUEST_TOTAL, KEY_VALUE_HEADS, group_width, HEAD_SIZE)
    query_change = adapter_change.reshape(REQUEST_TOTAL, KEY_VALUE_HEADS, group_width, HEAD_SIZE)
    result = lax.map(attend_one, (base_query, query_change, new_kv, cache_keys, cache_values, lengths))
    return result.reshape(REQUEST_TOTAL, MODEL_WIDTH)
```

```python
import functools
import math

import jax
import jax.numpy as jnp
from jax import lax
from jax.experimental import pallas as pl
from jax.experimental.pallas import tpu as pltpu
from jax.sharding import PartitionSpec as P

HEAD_SIZE = 128
CHIPS_Y = 4
LANES = 128
MESH = pl.DeviceIdType.MESH
NT = (((1,), (1,)), ((), ()))
NN = (((1,), (0,)), ((), ()))
VMEM_LIMIT = 56 * 1024 * 1024


def wait_bytes(ref, sem):
    pltpu.make_async_copy(ref, ref, sem).wait()


def delta_kernel(
    sizes,
    ids_ref,
    hidden_ref,
    down_ref,
    up_ref,
    out_ref,
    rows_in,
    ids_own,
    ids_in,
    downs,
    ups,
    picked,
    key_rows,
    odd_rows,
    partial,
    partial_in,
    low_own,
    low_in,
    delta,
    local_sem,
    rows_send,
    rows_recv,
    ids_send,
    ids_recv,
    slice_send,
    ring_send,
    ring_recv,
    partial_send,
    partial_recv,
    low_send,
    low_recv,
    delta_send,
    delta_recv,
):
    nx, ny, nz, nt = sizes
    plane = nx * ny
    team = plane * nt
    rows, width = hidden_ref.shape
    rank = down_ref.shape[0]
    part = width // plane
    total_rows = plane * rows
    half_rows = total_rows // 2
    blocks = ids_ref.shape[0]
    block_rows = rows // blocks
    pack = half_rows // team

    x = lax.axis_index("batch")
    pool = lax.axis_index("pool")
    t = lax.axis_index("tensor")
    z = pool // ny
    y = pool % ny
    slot = x * ny + y
    seat = slot * nt + t

    def at_slot(s):
        return (s // ny, z * ny + s % ny, t)

    def at_seat(q):
        return (q // (ny * nt), z * ny + (q // nt) % ny, q % nt)

    def at_z(zz):
        return (x, zz * ny + y, t)

    def columns(s):
        return pl.ds(pl.multiple_of(s * part, part), part)

    barrier = pltpu.get_barrier_semaphore()

    def greet(i, carry):
        pl.semaphore_signal(barrier, 1, device_id=at_seat((seat + i) % team), device_id_type=MESH)
        return carry

    lax.fori_loop(1, team, greet, 0)
    pl.semaphore_signal(barrier, 1, device_id=at_z((z + 1) % nz), device_id_type=MESH)
    pl.semaphore_signal(barrier, 1, device_id=at_z((z + nz - 1) % nz), device_id_type=MESH)

    block_iota = lax.broadcasted_iota(jnp.int32, (blocks, LANES), 0)
    named = jnp.zeros((blocks, LANES), jnp.int32)
    for b in range(blocks):
        named = jnp.where(block_iota == b, ids_ref[b], named)
    ids_own[...] = named.astype(jnp.float32).astype(jnp.bfloat16)
    ids_in[slot] = ids_own[...]

    own_rows = pltpu.make_async_copy(hidden_ref.at[:, columns(slot)], rows_in.at[slot], local_sem.at[0])
    own_rows.start()
    own_down = pltpu.make_async_copy(down_ref.at[:, columns(slot)], downs.at[z, y], local_sem.at[1])
    own_down.start()
    own_up = pltpu.make_async_copy(up_ref.at[:, columns(slot)], ups.at[z, y], local_sem.at[2])
    own_up.start()

    pl.semaphore_wait(barrier, team + 1)

    def ring_copy(kind, buffer, zz, yy, to, side):
        if side < 2:
            ref = buffer.at[zz, yy]
        else:
            ref = buffer.at[zz, yy, pl.ds((side - 2) * (rank // 2), rank // 2)]
        return pltpu.make_async_remote_copy(
            src_ref=ref,
            dst_ref=ref,
            send_sem=ring_send.at[kind],
            recv_sem=ring_recv.at[kind, zz, yy, max(side - 2, 0)],
            device_id=at_z(to),
            device_id_type=MESH,
        )

    right, left = (z + 1) % nz, (z + nz - 1) % nz
    full = nz // 2 - 1

    def slice_exchange(kind, source, buffer):
        def send(i, carry):
            yy = (y + i) % ny
            pltpu.make_async_remote_copy(
                src_ref=source.at[:, columns(x * ny + yy)],
                dst_ref=buffer.at[z, y],
                send_sem=slice_send.at[kind],
                recv_sem=ring_recv.at[kind, z, y, 0],
                device_id=(x, z * ny + yy, t),
                device_id_type=MESH,
            ).start()
            return carry

        lax.fori_loop(1, ny, send, 0)

    def ring_first(kind, buffer):
        def one(i, carry):
            yy = (y + i) % ny

            @pl.when(i > 0)
            def _():
                wait_bytes(buffer.at[z, yy], ring_recv.at[kind, z, yy, 0])

            ring_copy(kind, buffer, z, yy, right, 0).start()
            ring_copy(kind, buffer, z, yy, left, 1).start()
            return carry

        lax.fori_loop(0, ny, one, 0)

    def ring_step(kind, buffer, k):
        def one(i, carry):
            yy = (y + i) % ny
            for side, zz, to in ((0, (z + nz - k) % nz, right), (1, (z + k) % nz, left)):
                if k <= full:
                    wait_bytes(buffer.at[zz, yy], ring_recv.at[kind, zz, yy, 0])
                    ring_copy(kind, buffer, zz, yy, to, side if k < full else side + 2).start()
                else:
                    wait_bytes(
                        buffer.at[zz, yy, pl.ds(side * (rank // 2), rank // 2)],
                        ring_recv.at[kind, zz, yy, side],
                    )
            return carry

        lax.fori_loop(0, ny, one, 0)

    slice_exchange(0, down_ref, downs)

    def send_rows(i, carry):
        s = (slot + i) % plane
        pltpu.make_async_remote_copy(
            src_ref=ids_own,
            dst_ref=ids_in.at[slot],
            send_sem=ids_send,
            recv_sem=ids_recv,
            device_id=at_slot(s),
            device_id_type=MESH,
        ).start()
        pltpu.make_async_remote_copy(
            src_ref=hidden_ref.at[:, columns(s)],
            dst_ref=rows_in.at[slot],
            send_sem=rows_send,
            recv_sem=rows_recv,
            device_id=at_slot(s),
            device_id_type=MESH,
        ).start()
        return carry

    lax.fori_loop(1, plane, send_rows, 0)
    own_down.wait()
    ring_first(0, downs)
    slice_exchange(1, up_ref, ups)

    wait_bytes(ids_in.at[pl.ds(0, plane - 1)], ids_recv)
    spread = lax.broadcasted_iota(jnp.int32, (rows, blocks), 0) // block_rows == lax.broadcasted_iota(
        jnp.int32, (rows, blocks), 1
    )
    spread = jnp.where(spread, 1.0, 0.0).astype(jnp.bfloat16)

    def expand(s, carry):
        ids = lax.dot_general(spread, ids_in[s], NN, preferred_element_type=jnp.float32).astype(jnp.int32)
        at = pl.ds(pl.multiple_of(s * rows, rows), rows)
        key_rows[at, :] = ids // 2
        odd_rows[at, :] = ids % 2
        return carry

    lax.fori_loop(0, plane, expand, 0)

    own_rows.wait()
    wait_bytes(rows_in.at[pl.ds(0, plane - 1)], rows_recv)

    def use_down(zz, first):
        weights = downs[zz].reshape(ny * rank, part)

        def one(i, carry):
            lhs = rows_in[pl.ds(2 * i, 2)].reshape(2 * rows, part)
            product = lax.dot_general(lhs, weights, NT, preferred_element_type=jnp.float32)
            at = pl.ds(pl.multiple_of(i * 2 * rows, 2 * rows), 2 * rows)
            keys = key_rows[at, :]
            value = jnp.zeros((2 * rows, LANES), jnp.float32) if first else picked[at, :]
            for g in range(ny * rank // LANES):
                value = jnp.where(
                    keys == zz * (ny * rank // LANES) + g, product[:, g * LANES : (g + 1) * LANES], value
                )
            picked[at, :] = value
            return carry

        lax.fori_loop(0, plane // 2, one, 0)

    use_down(z, True)
    for k in range(1, full + 1):
        ring_step(0, downs, k)
        use_down((z + nz - k) % nz, False)
        use_down((z + k) % nz, False)
    own_up.wait()
    ring_first(1, ups)
    ring_step(0, downs, full + 1)
    use_down((z + full + 1) % nz, False)

    def fold(s, carry):
        both = []
        upper = lax.broadcasted_iota(jnp.int32, (rows, LANES), 1) // rank
        for h in range(2):
            at = pl.ds(pl.multiple_of(h * half_rows + s * rows, rows), rows)
            kept = jnp.where(odd_rows[at, :] == upper, picked[at, :], 0.0)
            both.append(kept + pltpu.roll(kept, rank, 1))
        partial[pl.ds(pl.multiple_of(s * rows, rows), rows), :] = jnp.where(upper == 0, both[0], both[1])
        return carry

    lax.fori_loop(0, plane // 2, fold, 0)

    def packed(q):
        return pl.ds(pl.multiple_of(q * pack, pack), pack)

    def send_partial(i, carry):
        q = (seat + i) % team
        pltpu.make_async_remote_copy(
            src_ref=partial.at[packed(q)],
            dst_ref=partial_in.at[seat],
            send_sem=partial_send,
            recv_sem=partial_recv,
            device_id=at_seat(q),
            device_id_type=MESH,
        ).start()
        return carry

    lax.fori_loop(1, team, send_partial, 0)
    partial_in[seat] = partial[packed(seat), :]
    ring_step(1, ups, 1)
    wait_bytes(partial_in.at[pl.ds(0, team - 1)], partial_recv)
    low = jnp.sum(partial_in[...], axis=0).astype(jnp.bfloat16)
    low_own[...] = low
    low_in[seat] = low

    def send_low(i, carry):
        pltpu.make_async_remote_copy(
            src_ref=low_own,
            dst_ref=low_in.at[seat],
            send_sem=low_send,
            recv_sem=low_recv,
            device_id=at_seat((seat + i) % team),
            device_id_type=MESH,
        ).start()
        return carry

    lax.fori_loop(1, team, send_low, 0)
    for k in range(2, full + 2):
        ring_step(1, ups, k)
    wait_bytes(low_in.at[pl.ds(0, team - 1)], low_recv)

    groups = nz * ny * rank // LANES

    def use_up(i, carry):
        p = (slot + i) % (plane // 2)
        per = rows // pack
        low = low_in[pl.ds(p * per, per)].reshape(rows, LANES).astype(jnp.float32)
        turned = pltpu.roll(low, rank, 1)
        upper = lax.broadcasted_iota(jnp.int32, (rows, LANES), 1) // rank
        doubled = (jnp.where(upper == 0, low, turned), jnp.where(upper == 0, turned, low))
        lhs = []
        for h in range(2):
            at = pl.ds(pl.multiple_of(h * half_rows + p * rows, rows), rows)
            kept = jnp.where(odd_rows[at, :] == upper, doubled[h], 0.0)
            keys = key_rows[at, :]
            lhs.append(
                jnp.concatenate([jnp.where(keys == g, kept, 0.0).astype(jnp.bfloat16) for g in range(groups)], axis=1)
            )
        lhs = jnp.concatenate(lhs, axis=0)
        result = lax.dot_general(
            lhs, ups[...].reshape(nz * ny * rank, part), NN, preferred_element_type=jnp.float32
        ).astype(jnp.bfloat16)
        for h in range(2):
            s = p + h * (plane // 2)
            delta[s] = result[h * rows : (h + 1) * rows]

            @pl.when(s == slot)
            def _():
                pltpu.make_async_copy(delta.at[s], out_ref.at[:, columns(slot)], local_sem.at[3]).start()

            @pl.when(s != slot)
            def _():
                pltpu.make_async_remote_copy(
                    src_ref=delta.at[s],
                    dst_ref=out_ref.at[:, columns(slot)],
                    send_sem=delta_send,
                    recv_sem=delta_recv,
                    device_id=at_slot(s),
                    device_id_type=MESH,
                ).start()

        return carry

    lax.fori_loop(0, plane // 2, use_up, 0)

    wait_bytes(delta.at[0], local_sem.at[3])
    wait_bytes(delta.at[pl.ds(0, plane - 1)], delta_recv)
    wait_bytes(delta.at[pl.ds(0, plane - 1)], delta_send)
    wait_bytes(rows_in.at[pl.ds(0, plane - 1)], rows_send)
    wait_bytes(ids_in.at[pl.ds(0, plane - 1)], ids_send)
    wait_bytes(partial_in.at[pl.ds(0, team - 1)], partial_send)
    wait_bytes(low_in.at[pl.ds(0, team - 1)], low_send)
    for kind, buffer in ((0, downs), (1, ups)):
        wait_bytes(buffer.at[0, pl.ds(0, ny - 1)], slice_send.at[kind])
        wait_bytes(buffer.at[pl.ds(0, 2 * full + 1)], ring_send.at[kind])


def adapter_delta(ids, hidden, down, up, sizes):
    nx, ny, nz, nt = sizes
    plane = nx * ny
    team = plane * nt
    rows, width = hidden.shape
    rank = down.shape[0]
    part = width // plane
    blocks = ids.shape[0]
    total = plane * rows
    pack = total // 2 // team
    bf16, f32, i32 = jnp.bfloat16, jnp.float32, jnp.int32
    dma = pltpu.SemaphoreType.DMA
    anywhere = pl.BlockSpec(memory_space=pl.ANY)
    return pl.pallas_call(
        functools.partial(delta_kernel, sizes),
        out_shape=jax.ShapeDtypeStruct((rows, width), bf16),
        in_specs=[pl.BlockSpec(memory_space=pltpu.SMEM), anywhere, anywhere, anywhere],
        out_specs=anywhere,
        scratch_shapes=[
            pltpu.VMEM((plane, rows, part), bf16),
            pltpu.VMEM((blocks, LANES), bf16),
            pltpu.VMEM((plane, blocks, LANES), bf16),
            pltpu.VMEM((nz, ny, rank, part), bf16),
            pltpu.VMEM((nz, ny, rank, part), bf16),
            pltpu.VMEM((total, LANES), f32),
            pltpu.VMEM((total, LANES), i32),
            pltpu.VMEM((total, LANES), i32),
            pltpu.VMEM((total // 2, LANES), f32),
            pltpu.VMEM((team, pack, LANES), f32),
            pltpu.VMEM((pack, LANES), bf16),
            pltpu.VMEM((team, pack, LANES), bf16),
            pltpu.VMEM((plane, rows, part), bf16),
            dma((4,)),
            dma,
            dma,
            dma,
            dma,
            dma((2,)),
            dma((2,)),
            dma((2, nz, ny, 2)),
            dma,
            dma,
            dma,
            dma,
            dma,
            dma,
        ],
        compiler_params=pltpu.CompilerParams(
            collective_id=0, has_side_effects=True, vmem_limit_bytes=VMEM_LIMIT
        ),
    )(ids, hidden, down, up)


def attend_kernel(lengths_ref, base_ref, delta_ref, fresh_ref, keys_ref, values_ref, out_ref):
    step = pl.program_id(0)
    rows = base_ref.shape[0]
    heads = keys_ref.shape[1]
    slots = keys_ref.shape[2]
    group = base_ref.shape[1] // (heads * HEAD_SIZE)
    eight = 8
    scale = 1.0 / math.sqrt(HEAD_SIZE)
    tall = group * eight
    request = lax.broadcasted_iota(jnp.int32, (tall, LANES), 0) % eight
    lane = lax.broadcasted_iota(jnp.int32, (tall, LANES), 1)
    pair = request // 2
    mine = lane // slots == request % 2
    place = lane % slots
    fresh_lane = jnp.logical_and(jnp.logical_not(mine), place == request)
    limits = []
    for u in range(rows // eight):
        limit = jnp.zeros((tall, LANES), jnp.int32)
        for i in range(eight):
            limit = jnp.where(request == i, lengths_ref[step * rows + u * eight + i], limit)
        limits.append(limit)
    blank = jnp.zeros((slots - eight, HEAD_SIZE), jnp.bfloat16)

    def stack(ref, u, h):
        wide = ref[:, h * group * HEAD_SIZE : (h + 1) * group * HEAD_SIZE].astype(jnp.float32)
        wide = wide[u * eight : (u + 1) * eight]
        return jnp.concatenate([wide[:, g * HEAD_SIZE : (g + 1) * HEAD_SIZE] for g in range(group)], axis=0)

    for h in range(heads):
        outs = []
        for u in range(rows // eight):
            queries = jnp.concatenate([stack(base_ref, u, h), stack(delta_ref, u, h)], axis=0).astype(jnp.bfloat16)
            of = slice(u * eight, (u + 1) * eight)
            new = []
            for i in range(2):
                first = (i * heads + h) * HEAD_SIZE
                rows_new = fresh_ref[:, first : first + HEAD_SIZE].astype(jnp.float32)[of].astype(jnp.bfloat16)
                new.append(jnp.concatenate([rows_new, blank, rows_new, blank], axis=0))
            keys = jnp.concatenate([keys_ref[of, h].reshape(eight * slots, HEAD_SIZE), new[0]], axis=0)
            values = jnp.concatenate([values_ref[of, h].reshape(eight * slots, HEAD_SIZE), new[1]], axis=0)
            scores = lax.dot_general(queries, keys, NT, preferred_element_type=jnp.float32)
            scores = (scores[:tall] + scores[tall:]) * scale
            chosen = scores[:, :LANES]
            for j in range(1, eight // 2):
                chosen = jnp.where(pair == j, scores[:, j * LANES : (j + 1) * LANES], chosen)
            valid = jnp.logical_and(mine, place < limits[u])
            chosen = jnp.where(valid, chosen, jnp.where(fresh_lane, scores[:, -LANES:], -1e30))
            top = jnp.max(chosen, axis=1, keepdims=True)
            raised = jnp.where(jnp.logical_or(valid, fresh_lane), jnp.exp(chosen - top), 0.0)
            weights = raised / jnp.sum(raised, axis=1, keepdims=True)
            cached = jnp.where(mine, weights, 0.0)
            parts = [jnp.where(pair == j, cached, 0.0) for j in range(eight // 2)]
            parts.append(jnp.where(mine, 0.0, weights))
            spread = jnp.concatenate(parts, axis=1).astype(jnp.bfloat16)
            outs.append(lax.dot_general(spread, values, NN, preferred_element_type=jnp.float32))
        for g in range(group):
            first = (h * group + g) * HEAD_SIZE
            block = jnp.concatenate([o[g * eight : (g + 1) * eight] for o in outs], axis=0)
            out_ref[:, first : first + HEAD_SIZE] = block.astype(jnp.bfloat16)


def attend(lengths, base, delta, fresh, keys, values):
    rows, width = base.shape
    heads, slots = keys.shape[1:3]
    step = 16
    cache = pl.BlockSpec((step, heads, slots, HEAD_SIZE), lambda i: (i, 0, 0, 0))
    flat = pl.BlockSpec((step, width), lambda i: (i, 0))
    return pl.pallas_call(
        attend_kernel,
        grid=(rows // step,),
        out_shape=jax.ShapeDtypeStruct((rows, width), jnp.bfloat16),
        in_specs=[
            pl.BlockSpec(memory_space=pltpu.SMEM),
            flat,
            flat,
            pl.BlockSpec((step, fresh.shape[1]), lambda i: (i, 0)),
            cache,
            cache,
        ],
        out_specs=flat,
        compiler_params=pltpu.CompilerParams(vmem_limit_bytes=VMEM_LIMIT),
    )(lengths, base, delta, fresh, keys, values)


def body(
    sizes,
    hidden,
    query_base,
    new_kv,
    cache_keys,
    cache_values,
    lengths,
    adapter_ids,
    adapter_down,
    adapter_up,
):
    down = jnp.swapaxes(adapter_down, 1, 2)[0]
    delta = adapter_delta(adapter_ids[:, 0], hidden, down, adapter_up[0], sizes)
    fresh = new_kv.reshape(new_kv.shape[0], -1)
    return attend(lengths, query_base, delta, fresh, cache_keys, cache_values)


def solution(mesh):
    in_specs = (
        P(("batch", "pool"), "tensor"),
        P(("batch", "pool"), "tensor"),
        P(("batch", "pool"), None, "tensor"),
        P(("batch", "pool"), "tensor", None, None),
        P(("batch", "pool"), "tensor", None, None),
        P(("batch", "pool")),
        P(("batch", "pool"), None),
        P("pool", "tensor", None),
        P("pool", None, "tensor"),
    )
    out_specs = P(("batch", "pool"), "tensor")
    pool = mesh.shape["pool"]
    sizes = (mesh.shape["batch"], CHIPS_Y, pool // CHIPS_Y, mesh.shape["tensor"])
    return jax.shard_map(
        functools.partial(body, sizes), mesh=mesh, in_specs=in_specs, out_specs=out_specs, check_vma=False
    )
```

```python
import functools
import math

import jax
import jax.numpy as jnp
from jax import lax
from jax.experimental import pallas as pl
from jax.experimental.pallas import tpu as pltpu
from jax.sharding import PartitionSpec as P

HEAD_SIZE = 128
CHIPS_Y = 4
LANES = 128
EIGHT = 8
MESH = pl.DeviceIdType.MESH
NT = (((1,), (1,)), ((), ()))
NN = (((1,), (0,)), ((), ()))
VMEM_LIMIT = 56 * 1024 * 1024


def wait_bytes(ref, sem):
    pltpu.make_async_copy(ref, ref, sem).wait()


def kernel(
    sizes,
    ids_ref,
    lengths_ref,
    hidden_ref,
    base_ref,
    fresh_ref,
    keys_ref,
    values_ref,
    down_ref,
    up_ref,
    out_ref,
    rows_in,
    ids_own,
    ids_in,
    downs,
    ups,
    picked,
    key_rows,
    odd_rows,
    partial,
    partner_in,
    reduced,
    partial_in,
    low_own,
    low_in,
    delta,
    delta_in,
    queries,
    fresh,
    new_keys,
    new_values,
    keys,
    values,
    scores_base,
    result,
    local_sem,
    out_sem,
    rows_send,
    rows_recv,
    ids_send,
    ids_recv,
    slice_send,
    ring_send,
    ring_recv,
    partner_send,
    partner_recv,
    partial_send,
    partial_recv,
    low_send,
    low_recv,
    delta_send,
    delta_recv,
):
    nx, ny, nz, nt = sizes
    plane = nx * ny
    team = plane * nt
    rows, width = hidden_ref.shape
    rank = down_ref.shape[0]
    part = width // plane
    half_rows = plane * rows // 2
    blocks = ids_ref.shape[0]
    block_rows = rows // blocks
    pack = half_rows // team
    heads, slots = keys_ref.shape[1:3]
    group = width // (heads * HEAD_SIZE)
    tall = group * EIGHT
    scale = 1.0 / math.sqrt(HEAD_SIZE)
    assert heads == nx and ny * part == group * HEAD_SIZE

    x = lax.axis_index("batch")
    pool = lax.axis_index("pool")
    t = lax.axis_index("tensor")
    z = pool // ny
    y = pool % ny
    slot = x * ny + y
    seat = t * plane + slot

    def columns(s):
        return pl.ds(pl.multiple_of(s * part, part), part)

    def peer(i):
        return (x + nx // 2 + i // ny) % nx, (y + ny // 2 + i) % ny

    myself = (nx - nx // 2) % nx * ny + (ny - ny // 2) % ny

    def each_peer(one):
        lax.fori_loop(0, myself, one, 0)
        lax.fori_loop(myself + 1, plane, one, 0)

    right, left = (z + 1) % nz, (z + nz - 1) % nz
    full = nz // 2 - 1

    barrier = pltpu.get_barrier_semaphore()

    def greet(i, carry):
        px, py = peer(i)
        for pt in range(nt):
            pl.semaphore_signal(barrier, 1, device_id=(px, z * ny + py, pt), device_id_type=MESH)
        return carry

    each_peer(greet)
    for other in range(1, nt):
        pl.semaphore_signal(barrier, 1, device_id=(x, pool, (t + other) % nt), device_id_type=MESH)
    for zz in (right, left):
        pl.semaphore_signal(barrier, 1, device_id=(x, zz * ny + y, t), device_id_type=MESH)

    local = [
        pltpu.make_async_copy(hidden_ref.at[:, columns(slot)], rows_in.at[slot], local_sem.at[0]),
        pltpu.make_async_copy(down_ref.at[:, columns(slot)], downs.at[z, y], local_sem.at[1]),
        pltpu.make_async_copy(up_ref.at[:, columns(slot)], ups.at[z, y], local_sem.at[2]),
        pltpu.make_async_copy(base_ref, queries, local_sem.at[3]),
        pltpu.make_async_copy(fresh_ref, fresh, local_sem.at[4]),
        pltpu.make_async_copy(keys_ref, keys, local_sem.at[5]),
        pltpu.make_async_copy(values_ref, values, local_sem.at[6]),
    ]
    for copy in (local[1], local[0], local[2]):
        copy.start()

    block_iota = lax.broadcasted_iota(jnp.int32, (blocks, LANES), 0)
    named = jnp.zeros((blocks, LANES), jnp.int32)
    for b in range(blocks):
        named = jnp.where(block_iota == b, ids_ref[b], named)
    ids_own[...] = named.astype(jnp.float32).astype(jnp.bfloat16)
    ids_in[slot] = ids_own[...]

    pl.semaphore_wait(barrier, team + 1)

    def slice_exchange(kind, source, buffer):
        def send(i, carry):
            yy = (y + i) % ny
            pltpu.make_async_remote_copy(
                src_ref=source.at[:, columns(x * ny + yy)],
                dst_ref=buffer.at[z, y],
                send_sem=slice_send.at[kind],
                recv_sem=ring_recv.at[kind, z, y, 0],
                device_id=(x, z * ny + yy, t),
                device_id_type=MESH,
            ).start()
            return carry

        lax.fori_loop(1, ny, send, 0)

    def ring_copy(kind, buffer, zz, yy, to, side):
        if side < 2:
            ref = buffer.at[zz, yy]
        else:
            ref = buffer.at[zz, yy, pl.ds((side - 2) * (rank // 2), rank // 2)]
        return pltpu.make_async_remote_copy(
            src_ref=ref,
            dst_ref=ref,
            send_sem=ring_send.at[kind],
            recv_sem=ring_recv.at[kind, zz, yy, max(side - 2, 0)],
            device_id=(x, to * ny + y, t),
            device_id_type=MESH,
        )

    def ring_own(kind, buffer):
        ring_copy(kind, buffer, z, y, right, 0).start()
        ring_copy(kind, buffer, z, y, left, 1).start()

    def ring_first(kind, buffer):
        def one(i, carry):
            yy = (y + i) % ny
            wait_bytes(buffer.at[z, yy], ring_recv.at[kind, z, yy, 0])
            ring_copy(kind, buffer, z, yy, right, 0).start()
            ring_copy(kind, buffer, z, yy, left, 1).start()
            return carry

        lax.fori_loop(1, ny, one, 0)

    def ring_step(kind, buffer, k, beside=None):
        def one(i, carry):
            yy = (y + i) % ny
            for side, zz, to in ((0, (z + nz - k) % nz, right), (1, (z + k) % nz, left)):
                if k <= full:
                    wait_bytes(buffer.at[zz, yy], ring_recv.at[kind, zz, yy, 0])
                    ring_copy(kind, buffer, zz, yy, to, side if k < full else side + 2).start()
                else:
                    wait_bytes(
                        buffer.at[zz, yy, pl.ds(side * (rank // 2), rank // 2)],
                        ring_recv.at[kind, zz, yy, side],
                    )
            if beside is not None:
                beside(i)
            return carry

        lax.fori_loop(0, ny, one, 0)

    slice_exchange(0, down_ref, downs)

    def send_rows(i, carry):
        px, py = peer(i)
        pltpu.make_async_remote_copy(
            src_ref=ids_own,
            dst_ref=ids_in.at[slot],
            send_sem=ids_send,
            recv_sem=ids_recv,
            device_id=(px, z * ny + py, t),
            device_id_type=MESH,
        ).start()
        pltpu.make_async_remote_copy(
            src_ref=hidden_ref.at[:, columns(px * ny + py)],
            dst_ref=rows_in.at[slot],
            send_sem=rows_send,
            recv_sem=rows_recv,
            device_id=(px, z * ny + py, t),
            device_id_type=MESH,
        ).start()
        return carry

    local[1].wait()
    ring_own(0, downs)
    each_peer(send_rows)
    slice_exchange(1, up_ref, ups)
    for copy in (local[3], local[4], local[5], local[6]):
        copy.start()
    ring_first(0, downs)

    local[4].wait()

    def unpack(i, carry):
        at = pl.ds(pl.multiple_of(i * EIGHT, EIGHT), EIGHT)
        wide = fresh[at].astype(jnp.float32)
        new_keys[at, :] = wide[:, 0, :]
        new_values[at, :] = wide[:, 1, :]
        return carry

    lax.fori_loop(0, rows // EIGHT, unpack, 0)
    ring_step(0, downs, 1)

    wait_bytes(ids_in.at[pl.ds(0, plane - 1)], ids_recv)
    spread = lax.broadcasted_iota(jnp.int32, (rows, blocks), 0) // block_rows == lax.broadcasted_iota(
        jnp.int32, (rows, blocks), 1
    )
    spread = jnp.where(spread, 1.0, 0.0).astype(jnp.bfloat16)

    def expand(s, carry):
        ids = lax.dot_general(spread, ids_in[s], NN, preferred_element_type=jnp.float32).astype(jnp.int32)
        at = pl.ds(pl.multiple_of(s * rows, rows), rows)
        key_rows[at, :] = ids // 2
        odd_rows[at, :] = ids % 2
        return carry

    lax.fori_loop(0, plane, expand, 0)
    local[0].wait()
    wait_bytes(rows_in.at[pl.ds(0, plane - 1)], rows_recv)

    per_chunk = ny * rank // LANES

    def use_down(i, chunks, first=False):
        lhs = rows_in[pl.ds(2 * i, 2)].reshape(2 * rows, part)
        at = pl.ds(pl.multiple_of(i * 2 * rows, 2 * rows), 2 * rows)
        named = key_rows[at, :]
        value = jnp.zeros((2 * rows, LANES), jnp.float32) if first else picked[at, :]
        for zz in chunks:
            product = lax.dot_general(
                lhs, downs[zz].reshape(ny * rank, part), NT, preferred_element_type=jnp.float32
            )
            for g in range(per_chunk):
                value = jnp.where(named == zz * per_chunk + g, product[:, g * LANES : (g + 1) * LANES], value)
        picked[at, :] = value

    def some_down(chunks, first=False):
        count = plane // 2 // ny

        def beside(i):
            for c in range(count):
                use_down(count * i + c, chunks, first)

        if plane // 2 % ny == 0:
            return beside, False
        return None, True

    def ring_and_down(k, chunks, first=False):
        beside, late = some_down(chunks, first)
        ring_step(0, downs, k, beside)
        if late:
            for i in range(plane // 2):
                use_down(i, chunks, first)

    near = [z, (z + nz - 1) % nz, (z + 1) % nz]
    for k in range(2, full + 1):
        ring_and_down(k, near if k == 2 else [(z + nz - k + 1) % nz, (z + k - 1) % nz], k == 2)
    local[2].wait()
    ring_own(1, ups)
    ring_first(1, ups)
    ring_and_down(full + 1, near if full == 1 else [(z + nz - full) % nz, (z + full) % nz], full == 1)

    def fold(u, carry):
        use_down(u, [(z + full + 1) % nz])
        upper = lax.broadcasted_iota(jnp.int32, (rows, LANES), 1) // rank
        both = []
        for h in range(2):
            at = pl.ds(pl.multiple_of((2 * u + h) * rows, rows), rows)
            kept = jnp.where(odd_rows[at, :] == upper, picked[at, :], 0.0)
            both.append(kept + pltpu.roll(kept, rank, 1))
        partial[pl.ds(pl.multiple_of(u * rows, rows), rows), :] = jnp.where(upper == 0, both[0], both[1])
        return carry

    lax.fori_loop(0, plane // 2, fold, 0)

    share = half_rows // nt

    def half_of(core):
        return pl.ds(pl.multiple_of(core * share, share), share)

    swap = pltpu.make_async_remote_copy(
        src_ref=partial.at[half_of(1 - t)],
        dst_ref=partner_in,
        send_sem=partner_send,
        recv_sem=partner_recv,
        device_id=(x, pool, 1 - t),
        device_id_type=MESH,
    )
    swap.start()
    swap.wait_recv()
    reduced[...] = partial[half_of(t), :] + partner_in[...]

    def packed(s):
        return pl.ds(pl.multiple_of(s * pack, pack), pack)

    def send_partial(i, carry):
        px, py = peer(i)
        pltpu.make_async_remote_copy(
            src_ref=reduced.at[packed(px * ny + py)],
            dst_ref=partial_in.at[slot],
            send_sem=partial_send,
            recv_sem=partial_recv,
            device_id=(px, z * ny + py, t),
            device_id_type=MESH,
        ).start()
        return carry

    each_peer(send_partial)
    partial_in[slot] = reduced[packed(slot), :]

    pairs = rows // (2 * EIGHT)
    request = lax.broadcasted_iota(jnp.int32, (1, EIGHT, LANES), 1)
    lane = lax.broadcasted_iota(jnp.int32, (1, EIGHT, LANES), 2)
    pair = request // 2
    mine = lane // slots == request % 2
    place = lane % slots
    fresh_lane = jnp.logical_and(jnp.logical_not(mine), place == request)
    pair_masks = [jnp.logical_and(mine, pair == j) for j in range(EIGHT // 2)]
    blank = jnp.zeros((slots - EIGHT, HEAD_SIZE), jnp.float32)

    def stacked(wide):
        return jnp.concatenate(wide, axis=0).astype(jnp.bfloat16)

    def fresh_tile(ref, at, h):
        new = ref[at, pl.ds(pl.multiple_of(h * HEAD_SIZE, HEAD_SIZE), HEAD_SIZE)]
        return jnp.concatenate([new, blank, new, blank], axis=0).astype(jnp.bfloat16)

    def chosen_scores(lhs, at, h):
        against = keys[at, h].reshape(EIGHT * slots, HEAD_SIZE)
        cached = lax.dot_general(lhs, against, NT, preferred_element_type=jnp.float32)
        new = lax.dot_general(lhs, fresh_tile(new_keys, at, h), NT, preferred_element_type=jnp.float32)
        chosen = new.reshape(group, EIGHT, LANES)
        for j in range(EIGHT // 2):
            tile = cached[:, j * LANES : (j + 1) * LANES].reshape(group, EIGHT, LANES)
            chosen = jnp.where(pair_masks[j], tile, chosen)
        return chosen * scale

    def base_scores(h, n):
        first = pl.multiple_of(n * 2 * EIGHT, 2 * EIGHT)
        wide = [
            queries[
                pl.ds(first, 2 * EIGHT),
                pl.ds(pl.multiple_of((h * group + g) * HEAD_SIZE, HEAD_SIZE), HEAD_SIZE),
            ].astype(jnp.float32)
            for g in range(group)
        ]
        for u in range(2):
            at = pl.ds(pl.multiple_of(first + u * EIGHT, EIGHT), EIGHT)
            lhs = stacked([w[u * EIGHT : (u + 1) * EIGHT] for w in wide])
            limit = jnp.zeros((1, EIGHT, LANES), jnp.int32)
            for i in range(EIGHT):
                limit = jnp.where(request == i, lengths_ref[first + u * EIGHT + i], limit)
            seen = jnp.logical_or(jnp.logical_and(mine, place < limit), fresh_lane)
            chosen = jnp.where(seen, chosen_scores(lhs, at, h), -1e30)
            scores_base[h, 2 * n + u] = chosen.reshape(tall, LANES)

    turns = (full + 1) * ny

    def beside_up(k):
        def beside(i):
            m = (k - 1) * ny + i
            if heads * pairs >= turns:
                base_scores(m // pairs, m % pairs)

        return beside

    local[3].wait()
    local[5].wait()
    ring_step(1, ups, 1, beside_up(1))
    wait_bytes(partial_in.at[pl.ds(0, plane - 1)], partial_recv)
    low = jnp.sum(partial_in[...], axis=0).astype(jnp.bfloat16)
    low_own[...] = low
    low_in[seat] = low

    def send_low_to(device):
        pltpu.make_async_remote_copy(
            src_ref=low_own,
            dst_ref=low_in.at[seat],
            send_sem=low_send,
            recv_sem=low_recv,
            device_id=device,
            device_id_type=MESH,
        ).start()

    def send_low(i, carry):
        px, py = peer(i)
        for pt in range(nt):
            send_low_to((px, z * ny + py, pt))
        return carry

    each_peer(send_low)
    send_low_to((x, pool, 1 - t))
    for k in range(2, full + 2):
        ring_step(1, ups, k, beside_up(k))
    for m in range(turns if heads * pairs >= turns else 0, heads * pairs):
        base_scores(m // pairs, m % pairs)
    wait_bytes(low_in.at[pl.ds(0, team - 1)], low_recv)

    groups = nz * ny * rank // LANES
    per = rows // pack

    def use_up(i, carry):
        px = (x + nx // 2 + i // (ny // 2)) % nx
        u = px * (ny // 2) + (y // 2 + 1 + i) % (ny // 2)
        low = low_in[pl.ds(u * per, per)].reshape(rows, LANES).astype(jnp.float32)
        turned = pltpu.roll(low, rank, 1)
        upper = lax.broadcasted_iota(jnp.int32, (rows, LANES), 1) // rank
        doubled = (jnp.where(upper == 0, low, turned), jnp.where(upper == 0, turned, low))
        lhs = []
        for h in range(2):
            at = pl.ds(pl.multiple_of((2 * u + h) * rows, rows), rows)
            kept = jnp.where(odd_rows[at, :] == upper, doubled[h], 0.0)
            named = key_rows[at, :]
            lhs.append(
                jnp.concatenate([jnp.where(named == g, kept, 0.0).astype(jnp.bfloat16) for g in range(groups)], axis=1)
            )
        change = lax.dot_general(
            jnp.concatenate(lhs, axis=0),
            ups[...].reshape(nz * ny * rank, part),
            NN,
            preferred_element_type=jnp.float32,
        ).astype(jnp.bfloat16)
        for h in range(2):
            s = 2 * u + h
            delta[s] = change[h * rows : (h + 1) * rows]

            @pl.when(s == slot)
            def _():
                delta_in[slot] = change[h * rows : (h + 1) * rows]

            @pl.when(s != slot)
            def _():
                pltpu.make_async_remote_copy(
                    src_ref=delta.at[s],
                    dst_ref=delta_in.at[slot],
                    send_sem=delta_send,
                    recv_sem=delta_recv.at[x],
                    device_id=(px, z * ny + s % ny, t),
                    device_id_type=MESH,
                ).start()

        return carry

    lax.fori_loop(0, plane // 2, use_up, 0)

    local[6].wait()
    per_part = part // HEAD_SIZE

    def head_columns(h):
        return pl.ds(pl.multiple_of(h * group * HEAD_SIZE, group * HEAD_SIZE), group * HEAD_SIZE)

    def attend(h, n):
        first = pl.multiple_of(n * 2 * EIGHT, 2 * EIGHT)
        wide = [
            delta_in[
                h * ny + g // per_part,
                pl.ds(first, 2 * EIGHT),
                g % per_part * HEAD_SIZE : (g % per_part + 1) * HEAD_SIZE,
            ].astype(jnp.float32)
            for g in range(group)
        ]
        outs = []
        for u in range(2):
            at = pl.ds(pl.multiple_of(first + u * EIGHT, EIGHT), EIGHT)
            lhs = stacked([w[u * EIGHT : (u + 1) * EIGHT] for w in wide])
            chosen = scores_base[h, 2 * n + u].reshape(group, EIGHT, LANES) + chosen_scores(lhs, at, h)
            raised = jnp.exp(chosen - jnp.max(chosen, axis=2, keepdims=True))
            total = jnp.sum(raised, axis=2, keepdims=True)
            cached = [jnp.where(m, raised, 0.0).reshape(tall, LANES) for m in pair_masks]
            new = jnp.where(mine, 0.0, raised).reshape(tall, LANES).astype(jnp.bfloat16)
            mixed = lax.dot_general(
                jnp.concatenate(cached, axis=1).astype(jnp.bfloat16),
                values[at, h].reshape(EIGHT * slots, HEAD_SIZE),
                NN,
                preferred_element_type=jnp.float32,
            ) + lax.dot_general(new, fresh_tile(new_values, at, h), NN, preferred_element_type=jnp.float32)
            outs.append((mixed.reshape(group, EIGHT, HEAD_SIZE) / total))
        for g in range(group):
            block = jnp.concatenate([o[g] for o in outs], axis=0)
            result[
                pl.ds(first, 2 * EIGHT), pl.ds(pl.multiple_of((h * group + g) * HEAD_SIZE, HEAD_SIZE), HEAD_SIZE)
            ] = block.astype(jnp.bfloat16)

    for j in range(nx):
        h = (x + nx - (nx // 2 + j) % nx) % nx
        arriving = ny - 1 if (nx // 2 + j) % nx == 0 else ny
        wait_bytes(delta_in.at[pl.ds(0, arriving)], delta_recv.at[h])

        def some(n, carry):
            attend(h, n)
            return carry

        lax.fori_loop(0, pairs, some, 0)
        pltpu.make_async_copy(result.at[:, head_columns(h)], out_ref.at[:, head_columns(h)], out_sem).start()

    wait_bytes(result, out_sem)
    wait_bytes(delta.at[pl.ds(0, plane - 1)], delta_send)
    wait_bytes(rows_in.at[pl.ds(0, plane - 1)], rows_send)
    wait_bytes(ids_in.at[pl.ds(0, plane - 1)], ids_send)
    swap.wait_send()
    wait_bytes(partial_in.at[pl.ds(0, plane - 1)], partial_send)
    wait_bytes(low_in.at[pl.ds(0, team - 1)], low_send)
    for kind, buffer in ((0, downs), (1, ups)):
        wait_bytes(buffer.at[0, pl.ds(0, ny - 1)], slice_send.at[kind])
        wait_bytes(buffer.at[pl.ds(0, 2 * full + 1)], ring_send.at[kind])


def body(
    sizes,
    hidden,
    query_base,
    new_kv,
    cache_keys,
    cache_values,
    lengths,
    adapter_ids,
    adapter_down,
    adapter_up,
):
    nx, ny, nz, nt = sizes
    plane = nx * ny
    team = plane * nt
    down = jnp.swapaxes(adapter_down, 1, 2)[0]
    up = adapter_up[0]
    rows, width = hidden.shape
    heads, slots = cache_keys.shape[1:3]
    rank = down.shape[0]
    part = width // plane
    blocks = adapter_ids.shape[0]
    total = plane * rows
    pack = total // 2 // team
    tall = width // (heads * HEAD_SIZE) * EIGHT
    bf16, f32, i32 = jnp.bfloat16, jnp.float32, jnp.int32
    dma = pltpu.SemaphoreType.DMA
    scalars = pl.BlockSpec(memory_space=pltpu.SMEM)
    anywhere = pl.BlockSpec(memory_space=pl.ANY)
    return pl.pallas_call(
        functools.partial(kernel, sizes),
        out_shape=jax.ShapeDtypeStruct((rows, width), bf16),
        in_specs=[scalars, scalars] + [anywhere] * 7,
        out_specs=anywhere,
        scratch_shapes=[
            pltpu.VMEM((plane, rows, part), bf16),
            pltpu.VMEM((blocks, LANES), bf16),
            pltpu.VMEM((plane, blocks, LANES), bf16),
            pltpu.VMEM((nz, ny, rank, part), bf16),
            pltpu.VMEM((nz, ny, rank, part), bf16),
            pltpu.VMEM((total, LANES), f32),
            pltpu.VMEM((total, LANES), i32),
            pltpu.VMEM((total, LANES), i32),
            pltpu.VMEM((total // 2, LANES), f32),
            pltpu.VMEM((total // 2 // nt, LANES), f32),
            pltpu.VMEM((total // 2 // nt, LANES), f32),
            pltpu.VMEM((plane, pack, LANES), f32),
            pltpu.VMEM((pack, LANES), bf16),
            pltpu.VMEM((team, pack, LANES), bf16),
            pltpu.VMEM((plane, rows, part), bf16),
            pltpu.VMEM((plane, rows, part), bf16),
            pltpu.VMEM((rows, width), bf16),
            pltpu.VMEM(new_kv.shape, bf16),
            pltpu.VMEM((rows, heads * HEAD_SIZE), f32),
            pltpu.VMEM((rows, heads * HEAD_SIZE), f32),
            pltpu.VMEM(cache_keys.shape, bf16),
            pltpu.VMEM(cache_values.shape, bf16),
            pltpu.VMEM((heads, rows // EIGHT, tall, LANES), f32),
            pltpu.VMEM((rows, width), bf16),
            dma((7,)),
            dma,
            dma,
            dma,
            dma,
            dma,
            dma((2,)),
            dma((2,)),
            dma((2, nz, ny, 2)),
            dma,
            dma,
            dma,
            dma,
            dma,
            dma,
            dma,
            dma((nx,)),
        ],
        compiler_params=pltpu.CompilerParams(
            collective_id=0, has_side_effects=True, vmem_limit_bytes=VMEM_LIMIT
        ),
    )(adapter_ids[:, 0], lengths, hidden, query_base, new_kv, cache_keys, cache_values, down, up)


def solution(mesh):
    in_specs = (
        P(("batch", "pool"), "tensor"),
        P(("batch", "pool"), "tensor"),
        P(("batch", "pool"), None, "tensor"),
        P(("batch", "pool"), "tensor", None, None),
        P(("batch", "pool"), "tensor", None, None),
        P(("batch", "pool")),
        P(("batch", "pool"), None),
        P("pool", "tensor", None),
        P("pool", None, "tensor"),
    )
    out_specs = P(("batch", "pool"), "tensor")
    pool = mesh.shape["pool"]
    sizes = (mesh.shape["batch"], CHIPS_Y, pool // CHIPS_Y, mesh.shape["tensor"])
    return jax.shard_map(
        functools.partial(body, sizes), mesh=mesh, in_specs=in_specs, out_specs=out_specs, check_vma=False
    )
```
